32 devices in a mesh: seq: 8 (over y, x, core), head: 4 (over z).
Axes of the slice: x: 2, y: 2, z: 4, core: 2. Of those that a mesh axis runs over, the one named last changes fastest.
Arguments:
- tokens: bfloat16 [8192, 1024], P(('seq', 'head')), may hold values from -6 to 6
- cotangent: bfloat16 [8192, 1024], P(('seq', 'head')), may hold values from -6 to 6
- image_counts: int32 [8, 9], P('seq'), may hold values from 6 to 896, as said below
- ln1_gain: float32 [1024], replicated, may hold values from 0.1 to 1.9
- ln1_bias: float32 [1024], replicated, may hold values from -3 to 3
- qkv_weight: bfloat16 [1024, 3072], replicated, may hold values from -0.1875 to 0.1875
- query_bias: float32 [1024], replicated, may hold values from -3 to 3
- value_bias: float32 [1024], replicated, may hold values from -3 to 3
- out_weight: bfloat16 [1024, 1024], replicated, may hold values from -0.75 to 0.75
- out_bias: float32 [1024], replicated, may hold values from -3 to 3
- scale_attn: float32 [1024], replicated, may hold values from 0.3 to 3
- ln2_gain: float32 [1024], replicated, may hold values from 0.1 to 1.9
- ln2_bias: float32 [1024], replicated, may hold values from -3 to 3
- up_weight: bfloat16 [1024, 4096], replicated, may hold values from -0.1875 to 0.1875
- up_bias: float32 [4096], replicated, may hold values from -3 to 3
- down_weight: bfloat16 [4096, 1024], replicated, may hold values from -0.09375 to 0.09375
- down_bias: float32 [1024], replicated, may hold values from -3 to 3
- scale_mlp: float32 [1024], replicated, may hold values from 0.3 to 3
Outputs:
- output: bfloat16 [8192, 1024], P(('seq', 'head'))
- tokens_grad: float32 [8192, 1024], P(('seq', 'head'))
- ln1_gain_grad: float32 [1024], P('seq')
- ln1_bias_grad: float32 [1024], P('seq')
- qkv_weight_grad: float32 [1024, 3072], P('seq')
- query_bias_grad: float32 [1024], P('seq')
- value_bias_grad: float32 [1024], P('seq')
- out_weight_grad: float32 [1024, 1024], P('seq')
- out_bias_grad: float32 [1024], P('seq')
- scale_attn_grad: float32 [1024], P('seq')
- ln2_gain_grad: float32 [1024], P('seq')
- ln2_bias_grad: float32 [1024], P('seq')
- up_weight_grad: float32 [1024, 4096], P('seq')
- up_bias_grad: float32 [4096], P('seq')
- down_weight_grad: float32 [4096, 1024], P('seq')
- down_bias_grad: float32 [1024], P('seq')
- scale_mlp_grad: float32 [1024], P('seq')
The draws below stay inside these ranges and needn't reach their ends.
Inputs may be any that keep to these rules, and one draw needn't show every extreme that they name: `image_counts`: row g lists the token counts of group g's 9 images in order and sums to 1024; image 4 (from 0) is the group's largest and holds at least 640 tokens; every image has 5 special tokens and one patch or more.
All inputs are finite; a program needn't handle non-finite values.
Results may differ from the reference program's by a relative error of at most 0.015.
Values may be sent and summed in bfloat16 or wider, within the bound.
No kernel may reach another device: no remote copies, remote signals or barrier semaphores. Data moves between devices by JAX's collectives and lax.ppermute only.
A program may use at most 192 MiB of HBM per device.

```python
import math
import jax
import jax.numpy as jnp
from jax import lax

D = 1024
HEADS = 16
HEAD_DIM = 64
FF = 4096
TOK_DEV = 256
SIDE_IMGS = 4
TOK_GROUP = 1024
GROUPS = 8
TOKENS = 8192


def split_total(key, totals, pieces, chosen):
    weights = jax.random.randint(key, (GROUPS, pieces), 1, 17) ** 3
    leftover = totals - 6 * pieces
    shares = leftover[:, None] * weights // jnp.sum(weights, 1, keepdims=True)
    if pieces > 1:
        shares = shares.at[chosen, pieces - 1].set(0)
    shares = shares.at[:, 0].add(leftover - jnp.sum(shares, 1))
    return shares + 6


def draw_image_counts(key, part):
    key = jax.random.fold_in(key, 7)
    key_before, key_after, key_front, key_rear, key_pick = jax.random.split(key, 5)
    lowest = TOK_DEV // 4
    highest = 3 * TOK_DEV // 4 + 1
    chosen = jax.random.randint(key_pick, (), 0, GROUPS)
    before = jax.random.randint(key_before, (GROUPS,), lowest, highest)
    after = jax.random.randint(key_after, (GROUPS,), lowest, highest)
    before = before.at[chosen].set(lowest)
    after = after.at[chosen].set(lowest)
    largest = TOK_GROUP - before - after
    front_counts = split_total(key_front, before, SIDE_IMGS, chosen)
    rear_counts = split_total(key_rear, after, SIDE_IMGS, chosen)
    return jnp.concatenate([front_counts, largest[:, None], rear_counts], 1).astype(jnp.int32)


def block_levels(stream_key, shape, shards, smallest, high):
    loudness = 1.0
    for dim, blocks in shards:
        heights = jax.random.uniform(jax.random.fold_in(jax.random.fold_in(stream_key, 6), dim), (blocks,), jnp.float32, smallest / len(shards), high / len(shards))
        loudness = loudness * jnp.repeat(jnp.exp(heights), shape[dim] // blocks).reshape((-1,) + (1,) * (len(shape) - 1 - dim))
    return loudness


def scatter_about(key, shape, scale, reach, cuts=(), kind=jnp.bfloat16):
    values = scale * jax.random.normal(key, shape, jnp.float32)
    if cuts:
        values = values * block_levels(key, shape, cuts, -0.22, 0.18)
    return jnp.clip(values, -reach, reach).astype(kind)


def setup_inputs(seed: int = 0) -> dict:
    key_of = jax.random.split(jax.random.key(seed), 19)
    return {
        "tokens": scatter_about(key_of[0], (TOKENS, D), 1.0, 6.0, ((0, 32),)),
        "cotangent": scatter_about(key_of[1], (TOKENS, D), 1.0, 6.0, ((0, 32),)),
        "image_counts": draw_image_counts(jax.random.fold_in(key_of[18], 71), 0),
        "ln1_gain": jnp.clip(1.0 + 0.18 * jax.random.normal(key_of[3], (D,), jnp.float32), 0.1, 1.9),
        "ln1_bias": scatter_about(key_of[4], (D,), 0.3, 3.0, (), jnp.float32),
        "qkv_weight": scatter_about(key_of[5], (D, 3 * D), D ** -0.5, 0.1875),
        "query_bias": scatter_about(key_of[6], (D,), 0.5, 3.0, (), jnp.float32),
        "value_bias": scatter_about(key_of[7], (D,), 0.5, 3.0, (), jnp.float32),
        "out_weight": scatter_about(key_of[8], (D, D), (D // 16) ** -0.5, 0.75),
        "out_bias": scatter_about(key_of[9], (D,), 0.3, 3.0, (), jnp.float32),
        "scale_attn": jnp.clip(jnp.exp(jax.random.uniform(key_of[10], (D,), jnp.float32, math.log(0.3), math.log(3.0))), 0.3, 3.0),
        "ln2_gain": jnp.clip(1.0 + 0.18 * jax.random.normal(key_of[11], (D,), jnp.float32), 0.1, 1.9),
        "ln2_bias": scatter_about(key_of[12], (D,), 0.3, 3.0, (), jnp.float32),
        "up_weight": scatter_about(key_of[13], (D, FF), D ** -0.5, 0.1875),
        "up_bias": scatter_about(key_of[14], (FF,), 0.5, 3.0, (), jnp.float32),
        "down_weight": scatter_about(key_of[15], (FF, D), FF ** -0.5, 0.09375),
        "down_bias": scatter_about(key_of[16], (D,), 0.3, 3.0, (), jnp.float32),
        "scale_mlp": jnp.clip(jnp.exp(jax.random.uniform(key_of[17], (D,), jnp.float32, math.log(0.3), math.log(3.0))), 0.3, 3.0),
    }


@jax.custom_vjp
def low(v):
    return lax.optimization_barrier(v.astype(jnp.bfloat16)).astype(jnp.float32)

@jax.custom_vjp
def low_back(v):
    return v

def low_keep(v):
    return (low(v), None)

def low_pass(kept, grad):
    return (grad,)

def back_keep(v):
    return (v, None)

def back_low(kept, grad):
    return (low(grad),)
low.defvjp(low_keep, low_pass)
low_back.defvjp(back_keep, back_low)
EPSILON = 1e-06
NEGATIVE = -1e+30

def layer_norm(values, scale_gain, shift_bias):
    average = lax.optimization_barrier(jnp.mean(values, -1, keepdims=True))
    centered = values - average
    variance = lax.optimization_barrier(jnp.mean(centered * centered, -1, keepdims=True))
    return centered * lax.rsqrt(variance + EPSILON) * scale_gain + shift_bias

def matmul(left, right):
    return jnp.dot(left, right, precision=lax.Precision.HIGHEST, preferred_element_type=jnp.float32)

def image_index(counts_row, length):
    boundary = jnp.cumsum(counts_row).astype(jnp.int32)
    places = jnp.arange(length, dtype=jnp.int32)
    return lax.optimization_barrier(jnp.sum((places[:, None] >= boundary[None, :]).astype(jnp.int32), 1))

def group_layer(params, rows, counts_row):
    ln1_gain, ln1_bias, qkv_weight, query_bias, value_bias, out_weight, out_bias, scale_attn, ln2_gain, ln2_bias, up_weight, up_bias, down_weight, down_bias, scale_mlp = params
    length = rows.shape[0]
    normed1 = low(layer_norm(rows, ln1_gain, ln1_bias))
    qkv_bias = jnp.concatenate([query_bias, jnp.zeros_like(query_bias), value_bias])
    projected = low(low_back(matmul(normed1, qkv_weight) + qkv_bias))
    queries = projected[:, :D].reshape(length, HEADS, HEAD_DIM)
    keys = projected[:, D:2 * D].reshape(length, HEADS, HEAD_DIM)
    values = projected[:, 2 * D:].reshape(length, HEADS, HEAD_DIM)
    labels = image_index(counts_row, length)
    block = min(512, length)
    factor = HEAD_DIM ** (-0.5)

    def one_block(number):
        start = number * block
        query_rows = lax.dynamic_slice_in_dim(queries, start, block, 0)
        query_labels = lax.dynamic_slice_in_dim(labels, start, block, 0)
        scores = jnp.einsum('qhd,khd->hqk', query_rows, keys, precision=lax.Precision.HIGHEST) * factor
        scores = jnp.where((query_labels[:, None] == labels[None, :])[None], scores, NEGATIVE)
        scores = low_back(scores)
        probs = low(jax.nn.softmax(scores, -1))
        return jnp.einsum('hqk,khd->qhd', probs, values, precision=lax.Precision.HIGHEST)
    mixed = lax.map(jax.checkpoint(one_block), jnp.arange(length // block, dtype=jnp.int32))
    mixed = low(low_back(mixed.reshape(length, D)))
    attended = low_back(matmul(mixed, out_weight) + out_bias)
    middle = rows + scale_attn * attended
    normed2 = low(layer_norm(middle, ln2_gain, ln2_bias))
    upward = low_back(matmul(normed2, up_weight) + up_bias)
    active = low(jax.nn.gelu(upward, approximate=False))
    downward = low_back(matmul(active, down_weight) + down_bias)
    return middle + scale_mlp * downward

def reference(tokens, cotangent, image_counts, ln1_gain, ln1_bias, qkv_weight, query_bias, value_bias, out_weight, out_bias, scale_attn, ln2_gain, ln2_bias, up_weight, up_bias, down_weight, down_bias, scale_mlp):
    params = tuple((item.astype(jnp.float32) for item in (ln1_gain, ln1_bias, qkv_weight, query_bias, value_bias, out_weight, out_bias, scale_attn, ln2_gain, ln2_bias, up_weight, up_bias, down_weight, down_bias, scale_mlp)))

    def whole(inputs, *weights):
        grouped = inputs.reshape(GROUPS, TOK_GROUP, D)

        def one_group(item):
            return group_layer(weights, item[0], item[1])
        result = lax.map(jax.checkpoint(one_group), (grouped, image_counts))
        return result.reshape(TOKENS, D)
    result, backward = jax.vjp(whole, tokens.astype(jnp.float32), *params)
    grads = backward(cotangent.astype(jnp.float32))
    return (result.astype(jnp.bfloat16), grads[0], grads[1], grads[2], grads[3], grads[4], grads[5], grads[6], grads[7], grads[8], grads[9], grads[10], grads[11], grads[12], grads[13], grads[14], grads[15])
```

```python
import functools
import math

import jax
import jax.numpy as jnp
from jax import lax
from jax.experimental import pallas as pl
from jax.experimental.pallas import tpu as pltpu
from jax.sharding import PartitionSpec as P

HEAD_DIM = 64
EPSILON = 1e-06
NEGATIVE = -1e30
MIB = 1024 * 1024
F32 = jnp.float32
BF16 = jnp.bfloat16


def dot_nn(left, right):
    return lax.dot_general(left, right, (((1,), (0,)), ((), ())), preferred_element_type=F32)


def dot_nt(left, right):
    return lax.dot_general(left, right, (((1,), (1,)), ((), ())), preferred_element_type=F32)


def dot_tn(left, right):
    return lax.dot_general(left, right, (((0,), (0,)), ((), ())), preferred_element_type=F32)


def unit_norm(values):
    average = jnp.mean(values, -1, keepdims=True)
    centered = values - average
    inverse = lax.rsqrt(jnp.mean(centered * centered, -1, keepdims=True) + EPSILON)
    return centered * inverse, inverse


def norm_back(grad_unit, unit_rows, inverse):
    first_term = jnp.mean(grad_unit, -1, keepdims=True)
    second_term = jnp.mean(grad_unit * unit_rows, -1, keepdims=True)
    return inverse * (grad_unit - first_term - unit_rows * second_term)


def column_sum(values):
    return jnp.sum(values, 0, keepdims=True)


def head_mask(rows, half):
    lane = lax.broadcasted_iota(jnp.int32, (rows, 2 * HEAD_DIM), 1)
    return (lane >= half * HEAD_DIM) & (lane < (half + 1) * HEAD_DIM)


def call(kernel, grid, scalars, in_specs, out_specs, out_shape, scratch, flops, nbytes, vmem=40):
    return pl.pallas_call(
        kernel,
        grid_spec=pltpu.PrefetchScalarGridSpec(
            num_scalar_prefetch=scalars,
            grid=grid,
            in_specs=in_specs,
            out_specs=out_specs,
            scratch_shapes=scratch,
        ),
        out_shape=out_shape,
        compiler_params=pltpu.CompilerParams(vmem_limit_bytes=vmem * MIB),
        cost_estimate=pl.CostEstimate(flops=flops, bytes_accessed=nbytes, transcendentals=0),
    )


def const(shape):
    zeros = (0,) * len(shape)
    return pl.BlockSpec(shape, lambda *_: zeros)


def qkv_kernel(where, tok, gain, bias, wq, wk, wv, bq, bv, qkv, unit):
    rows, _ = unit_norm(tok[...].astype(F32))
    unit[...] = rows.astype(BF16)
    normed = (rows * gain[...] + bias[...]).astype(BF16)
    wide = wq.shape[1]
    qkv[:, :wide] = (dot_nn(normed, wq[...]) + bq[...]).astype(BF16)
    qkv[:, wide : 2 * wide] = dot_nn(normed, wk[...]).astype(BF16)
    qkv[:, 2 * wide :] = (dot_nn(normed, wv[...]) + bv[...]).astype(BF16)


def qkv_forward(order, tokens_all, gain, bias, weight, query_bias, value_bias, heads, rows):
    length, width = tokens_all.shape
    wide = width // heads
    column = lambda part: pl.BlockSpec((width, wide), lambda k, o: (0, part * heads + o[0]))
    return call(
        qkv_kernel,
        (length // rows,),
        1,
        [
            pl.BlockSpec((rows, width), lambda k, o: (k, 0)),
            const((1, width)),
            const((1, width)),
            column(0),
            column(1),
            column(2),
            pl.BlockSpec((1, wide), lambda k, o: (0, o[0])),
            pl.BlockSpec((1, wide), lambda k, o: (0, o[0])),
        ],
        [
            pl.BlockSpec((rows, 3 * wide), lambda k, o: (k, 0)),
            pl.BlockSpec((rows, width), lambda k, o: (k, 0)),
        ],
        [
            jax.ShapeDtypeStruct((length, 3 * wide), BF16),
            jax.ShapeDtypeStruct((length, width), BF16),
        ],
        [],
        6 * length * width * wide,
        length * width * 8,
    )(order, tokens_all, gain, bias, weight, weight, weight, query_bias, value_bias)


def attend_kernel(order, q_ref, k_ref, v_ref, lab_q, lab_k, mixed, lse):
    rows, wide = q_ref.shape
    bias = jnp.where(lab_q[...] == lab_k[...], 0.0, NEGATIVE)
    for pair in range(wide // 128):
        lanes = slice(pair * 128, pair * 128 + 128)
        keys = k_ref[:, lanes]
        values = v_ref[:, lanes]
        queries = q_ref[:, lanes].astype(F32) * (HEAD_DIM**-0.5)
        done = []
        for half in range(2):
            own = jnp.where(head_mask(rows, half), queries, 0.0).astype(BF16)
            scores = dot_nt(own, keys) + bias
            highest = jnp.max(scores, -1, keepdims=True)
            weights = jnp.exp(scores - highest)
            total = jnp.sum(weights, -1, keepdims=True)
            done.append(dot_nn(weights.astype(BF16), values) / total)
            logsum = highest + jnp.log(total)
            spread = jnp.transpose(jnp.broadcast_to(logsum, (rows, 128)))
            lse[0, pl.ds(2 * pair + half, 1), :] = spread[0:1, :]
        mixed[0, :, lanes] = jnp.where(head_mask(rows, 0), done[0], done[1]).astype(BF16)


def attend(order, qkv, lab_col, lab_row, heads, rows):
    length = qkv.shape[0]
    wide = qkv.shape[1] // 3
    return call(
        attend_kernel,
        (heads,),
        1,
        [
            pl.BlockSpec((rows, wide), lambda k, o: (o[k], 0)),
            pl.BlockSpec((length, wide), lambda k, o: (0, 1)),
            pl.BlockSpec((length, wide), lambda k, o: (0, 2)),
            pl.BlockSpec((rows, 1), lambda k, o: (o[k], 0)),
            const((1, length)),
        ],
        [
            pl.BlockSpec((1, rows, wide), lambda k, o: (k, 0, 0)),
            pl.BlockSpec((1, 8, rows), lambda k, o: (k, 0, 0)),
        ],
        [
            jax.ShapeDtypeStruct((heads, rows, wide), BF16),
            jax.ShapeDtypeStruct((heads, 8, rows), F32),
        ],
        [],
        16 * length * length * wide,
        length * wide * 10,
    )(order, qkv, qkv, qkv, lab_col, lab_row)


def project_kernel(heads, order, *refs):
    pieces = refs[:heads]
    tok, out_w, out_b, scale, gain, bias, mixed, attended, middle, normed, total, piece = refs[heads:]
    k = pl.program_id(0)
    for j in range(heads):

        @pl.when(k == j)
        def _():
            piece[...] = pieces[j][...].reshape(piece.shape)

    mixed[...] = piece[...]
    part = dot_nn(piece[...], out_w[...])

    @pl.when(k == 0)
    def _():
        total[...] = part

    @pl.when(k > 0)
    def _():
        total[...] += part

    @pl.when(k == heads - 1)
    def _():
        result = total[...] + out_b[...]
        attended[...] = result
        after = tok[...].astype(F32) + scale[...] * result
        middle[...] = after
        normed[...] = (unit_norm(after)[0] * gain[...] + bias[...]).astype(BF16)


def project(order, mixed_x, received, tokens, out_weight, out_bias, scale, gain, bias):
    heads, rows, wide = mixed_x.shape
    width = tokens.shape[1]
    flat = const((rows, width))
    vector = const((1, width))
    return call(
        functools.partial(project_kernel, heads),
        (heads,),
        1,
        [const((1, rows, wide))]
        + [const((rows, wide))] * (heads - 1)
        + [flat, pl.BlockSpec((wide, width), lambda k, o: (o[k], 0))]
        + [vector] * 4,
        [pl.BlockSpec((rows, wide), lambda k, o: (0, o[k])), flat, flat, flat],
        [
            jax.ShapeDtypeStruct((rows, width), BF16),
            jax.ShapeDtypeStruct((rows, width), F32),
            jax.ShapeDtypeStruct((rows, width), F32),
            jax.ShapeDtypeStruct((rows, width), BF16),
        ],
        [pltpu.VMEM((rows, width), F32), pltpu.VMEM((rows, wide), BF16)],
        2 * rows * width * width,
        width * width * 2 + rows * width * 14,
    )(order, mixed_x, *received, tokens, out_weight, out_bias, scale, gain, bias)


def gelu_parts(values):
    size = jnp.abs(values)
    t = 1.0 / (1.0 + (0.3275911 / math.sqrt(2.0)) * size)
    bell = jnp.exp(-0.5 * values * values)
    poly = 0.5 * 1.061405429
    for term in (-1.453152027, 1.421413741, -0.284496736, 0.254829592):
        poly = poly * t + 0.5 * term
    tail = poly * t * bell
    share = jnp.where(values >= 0, 1.0 - tail, tail)
    slope = share + values * bell * (1.0 / math.sqrt(2.0 * math.pi))
    return values * share, slope


def ffn_kernel(core, n_own, n_other, g_own, g_other, up, up_b, down, down_out, grad_out, up_g, down_g, bias_g, rows_in, rows_t, grads):
    step = pl.program_id(0)
    rows = n_own.shape[0]

    @pl.when(step == 0)
    def _():
        rows_in[:rows] = n_own[...]
        rows_in[rows:] = n_other[...]
        rows_t[:, :rows] = jnp.transpose(n_own[...])
        rows_t[:, rows:] = jnp.transpose(n_other[...])
        grads[:rows] = g_own[...]
        grads[rows:] = g_other[...]

    upward = dot_nn(rows_in[...], up[...]) + up_b[...]
    active, slope = gelu_parts(upward)
    active = active.astype(BF16)
    grad_active = dot_nt(grads[...], down[...])
    grad_up = (grad_active * slope).astype(BF16)
    bias_g[...] = jnp.broadcast_to(column_sum(grad_up.astype(F32)), bias_g.shape)
    downward = dot_nn(active, down[...])
    grad_rows = dot_nt(grad_up, up[...])

    @pl.when(step == 0)
    def _():
        down_out[...] = downward
        grad_out[...] = grad_rows

    @pl.when(step > 0)
    def _():
        down_out[...] += downward
        grad_out[...] += grad_rows

    down_g[...] = dot_tn(active, grads[...]).astype(BF16)
    up_g[...] = dot_nn(rows_t[...], grad_up).astype(BF16)


def ffn(core, n_own, n_other, g_own, g_other, up, up_bias, down, blocks, block):
    rows, width = n_own.shape
    flat = const((rows, width))
    both = const((2 * rows, width))
    return call(
        ffn_kernel,
        (blocks,),
        1,
        [
            flat,
            flat,
            flat,
            flat,
            pl.BlockSpec((width, block), lambda i, c: (0, 2 * i + c[0])),
            pl.BlockSpec((1, block), lambda i, c: (0, 2 * i + c[0])),
            pl.BlockSpec((block, width), lambda i, c: (2 * i + c[0], 0)),
        ],
        [
            both,
            both,
            pl.BlockSpec((width, block), lambda i, c: (0, i)),
            pl.BlockSpec((block, width), lambda i, c: (i, 0)),
            pl.BlockSpec((8, block), lambda i, c: (0, i)),
        ],
        [
            jax.ShapeDtypeStruct((2 * rows, width), F32),
            jax.ShapeDtypeStruct((2 * rows, width), F32),
            jax.ShapeDtypeStruct((width, blocks * block), BF16),
            jax.ShapeDtypeStruct((blocks * block, width), BF16),
            jax.ShapeDtypeStruct((8, blocks * block), F32),
        ],
        [
            pltpu.VMEM((2 * rows, width), BF16),
            pltpu.VMEM((width, 2 * rows), BF16),
            pltpu.VMEM((2 * rows, width), BF16),
        ],
        12 * 2 * rows * width * blocks * block,
        width * blocks * block * 8 + rows * width * 20,
        50,
    )(core, n_own, n_other, g_own, g_other, up, up_bias, down)


def middle_kernel(heads, order, own, other, cot, middle, attended, gain, scale, out_w, grad_mid, grad_att, sums, pieces):
    k = pl.program_id(0)

    @pl.when(k == 0)
    def _():
        grad_rows = own[...] + other[...]
        unit, inverse = unit_norm(middle[...])
        result = cot[...].astype(F32) + norm_back(grad_rows * gain[...], unit, inverse)
        grad_mid[...] = result
        low = (scale[...] * result).astype(BF16)
        grad_att[...] = low
        sums[0:1] = column_sum(grad_rows * unit)
        sums[1:2] = column_sum(grad_rows)
        sums[2:3] = column_sum(result * attended[...])
        sums[3:4] = column_sum(low.astype(F32))
        sums[4:8] = jnp.zeros((4, sums.shape[1]), F32)

    pieces[0] = dot_nt(grad_att[...], out_w[...]).astype(BF16)


def middle_back(order, own, other, cot, middle, attended, gain, scale, out_weight, heads):
    rows, width = cot.shape
    wide = width // heads
    flat = const((rows, width))
    vector = const((1, width))
    return call(
        functools.partial(middle_kernel, heads),
        (heads,),
        1,
        [flat] * 5 + [vector] * 2 + [pl.BlockSpec((wide, width), lambda k, o: (o[k], 0))],
        [flat, flat, const((8, width)), pl.BlockSpec((1, rows, wide), lambda k, o: (k, 0, 0))],
        [
            jax.ShapeDtypeStruct((rows, width), F32),
            jax.ShapeDtypeStruct((rows, width), BF16),
            jax.ShapeDtypeStruct((8, width), F32),
            jax.ShapeDtypeStruct((heads, rows, wide), BF16),
        ],
        [],
        2 * rows * width * width,
        width * width * 2 + rows * width * 24,
    )(order, own, other, cot, middle, attended, gain, scale, out_weight)


def attend_back_kernel(heads, order, *refs):
    pieces = refs[:heads]
    q_ref, k_ref, v_ref, mixed, lse, lab_k, lab_q, grad, sums, grad_k, grad_v, rows_g = refs[heads:]
    step = pl.program_id(0)
    rows, wide = q_ref.shape
    length = k_ref.shape[0]
    chunk = min(256, length)
    for j in range(heads):

        @pl.when(step == j)
        def _():
            rows_g[...] = pieces[j][...].reshape(rows_g.shape)

    @pl.when(step == 0)
    def _():
        grad_k[...] = jnp.zeros_like(grad_k)
        grad_v[...] = jnp.zeros_like(grad_v)

    start = pl.multiple_of(order[step] * rows, rows)
    ones = jnp.ones((8, 128), F32)
    for pair in range(wide // 128):
        lanes = slice(pair * 128, pair * 128 + 128)
        queries = q_ref[:, lanes].astype(F32) * (HEAD_DIM**-0.5)
        grad_rows = rows_g[:, lanes].astype(F32)
        product = grad_rows * mixed[0, :, lanes].astype(F32)
        done = []
        for half in range(2):
            mask = head_mask(rows, half)
            own_q = jnp.where(mask, queries, 0.0).astype(BF16)
            own_g = jnp.where(mask, grad_rows, 0.0).astype(BF16)
            balance = lax.dot_general(
                ones,
                jnp.where(mask, product, 0.0),
                (((1,), (1,)), ((), ())),
                precision=lax.Precision.HIGHEST,
                preferred_element_type=F32,
            )[0:1]
            logsum = lse[0, pl.ds(2 * pair + half, 1), :]
            grad_q = jnp.zeros((rows, 128), F32)
            for part in range(length // chunk):
                here = slice(part * chunk, part * chunk + chunk)
                same = lab_k[here, :] == lab_q[...]
                scores = dot_nt(k_ref[here, lanes], own_q)
                probs = jnp.exp(jnp.where(same, scores - logsum, NEGATIVE))
                grad_probs = dot_nt(v_ref[here, lanes], own_g)
                grad_scores = (probs * (grad_probs - balance)).astype(BF16)
                grad_v[here, lanes] += dot_nn(probs.astype(BF16), own_g)
                grad_k[here, lanes] += dot_nn(grad_scores, own_q)
                grad_q += dot_tn(grad_scores, k_ref[here, lanes])
            done.append(grad_q * (HEAD_DIM**-0.5))
        grad[pl.ds(start, rows), lanes] = jnp.where(head_mask(rows, 0), done[0], done[1]).astype(BF16)

    @pl.when(step == heads - 1)
    def _():
        grad[:, wide : 2 * wide] = grad_k[...].astype(BF16)
        grad[:, 2 * wide :] = grad_v[...].astype(BF16)
        sums[...] = jnp.broadcast_to(column_sum(grad[...].astype(F32)), sums.shape)


def attend_back(order, own_x, received, qkv, mixed_x, lse, lab_col, lab_row):
    heads, rows, wide = mixed_x.shape
    length = qkv.shape[0]
    return call(
        functools.partial(attend_back_kernel, heads),
        (heads,),
        1,
        [const((1, rows, wide))]
        + [const((rows, wide))] * (heads - 1)
        + [
            pl.BlockSpec((rows, wide), lambda k, o: (o[k], 0)),
            pl.BlockSpec((length, wide), lambda k, o: (0, 1)),
            pl.BlockSpec((length, wide), lambda k, o: (0, 2)),
            pl.BlockSpec((1, rows, wide), lambda k, o: (k, 0, 0)),
            pl.BlockSpec((1, 8, rows), lambda k, o: (k, 0, 0)),
            const((length, 1)),
            pl.BlockSpec((1, rows), lambda k, o: (0, o[k])),
        ],
        [const((length, 3 * wide)), const((8, 3 * wide))],
        [
            jax.ShapeDtypeStruct((length, 3 * wide), BF16),
            jax.ShapeDtypeStruct((8, 3 * wide), F32),
        ],
        [
            pltpu.VMEM((length, wide), F32),
            pltpu.VMEM((length, wide), F32),
            pltpu.VMEM((rows, wide), BF16),
        ],
        40 * length * length * wide,
        length * wide * 20,
    )(order, own_x, *received, qkv, qkv, qkv, mixed_x, lse, lab_col, lab_row)


def qkv_grad_kernel(slots, order, unit, grad, wq, wk, wv, gain, bias, sums, small, packed):
    wide = wq.shape[1]
    rows = unit.shape[1]
    product = dot_tn(unit[...], grad[...])
    totals = sums[0:1, :]
    packed[:, : 3 * wide] = (gain[...] * product + bias[...] * totals).astype(BF16)
    gain_g = jnp.zeros((rows, 1), F32)
    bias_g = jnp.zeros((rows, 1), F32)
    for part, weight in enumerate((wq, wk, wv)):
        here = slice(part * wide, part * wide + wide)
        weights = weight[...].astype(F32)
        gain_g += jnp.sum(product[:, here] * weights, -1, keepdims=True)
        bias_g += jnp.sum(totals[:, here] * weights, -1, keepdims=True)
    columns = jnp.transpose(small[...])
    lane = lax.broadcasted_iota(jnp.int32, columns.shape, 1)
    columns = jnp.where(lane == slots, gain_g, jnp.where(lane == slots + 1, bias_g, columns))
    packed[:, 3 * wide :] = columns.astype(BF16)


def qkv_grad(order, unit, grad, weight, gain, bias, sums, small, slots, heads):
    length, width = unit.shape
    wide = width // heads
    rows = 256
    column = lambda part: pl.BlockSpec((rows, wide), lambda k, o: (k, part * heads + o[0]))
    return call(
        functools.partial(qkv_grad_kernel, slots),
        (width // rows,),
        1,
        [
            pl.BlockSpec((length, rows), lambda k, o: (0, k)),
            const((length, 3 * wide)),
            column(0),
            column(1),
            column(2),
            pl.BlockSpec((rows, 1), lambda k, o: (k, 0)),
            pl.BlockSpec((rows, 1), lambda k, o: (k, 0)),
            const((8, 3 * wide)),
            pl.BlockSpec((128, rows), lambda k, o: (0, k)),
        ],
        [pl.BlockSpec((rows, 3 * wide + 128), lambda k, o: (k, 0))],
        [jax.ShapeDtypeStruct((width, 3 * wide + 128), BF16)],
        [],
        6 * length * width * wide,
        length * width * 2 + length * wide * 6 + width * wide * 14,
    )(order, unit, grad, weight, weight, weight, gain, bias, sums, small)[0]


def input_kernel(heads, order, *refs):
    pieces = refs[:heads]
    wq, wk, wv, tok, gain, grad_mid, out, total, piece = refs[heads:]
    k = pl.program_id(0)
    wide = wq.shape[1]
    for j in range(heads):

        @pl.when(k == j)
        def _():
            piece[...] = pieces[j][...]

    part = dot_nt(piece[:, :wide], wq[...])
    part += dot_nt(piece[:, wide : 2 * wide], wk[...])
    part += dot_nt(piece[:, 2 * wide :], wv[...])

    @pl.when(k == 0)
    def _():
        total[...] = part

    @pl.when(k > 0)
    def _():
        total[...] += part

    @pl.when(k == heads - 1)
    def _():
        unit, inverse = unit_norm(tok[...].astype(F32))
        out[...] = grad_mid[...] + norm_back(total[...] * gain[...], unit, inverse)


def input_back(order, grad, received, weight, tokens, gain, grad_mid, heads):
    rows, width = tokens.shape
    wide = width // heads
    flat = const((rows, width))
    column = lambda part: pl.BlockSpec((width, wide), lambda k, o: (0, part * heads + o[k]))
    return call(
        functools.partial(input_kernel, heads),
        (heads,),
        1,
        [pl.BlockSpec((rows, 3 * wide), lambda k, o: (o[0], 0))]
        + [const((rows, 3 * wide))] * (heads - 1)
        + [column(0), column(1), column(2), flat, const((1, width)), flat],
        [flat],
        [jax.ShapeDtypeStruct((rows, width), F32)],
        [pltpu.VMEM((rows, width), F32), pltpu.VMEM((rows, 3 * wide), BF16)],
        6 * rows * width * width,
        width * width * 6 + rows * width * 16,
    )(order, grad, *received, weight, weight, weight, tokens, gain, grad_mid)[0]


def exchange(value, axis, distance):
    size = lax.axis_size(axis)
    return lax.ppermute(value, axis, [(i, i ^ distance) for i in range(size)])


def pick(stacked, index):
    return lax.dynamic_index_in_dim(stacked, index, 0, keepdims=False)


def body(
    tokens,
    cotangent,
    image_counts,
    ln1_gain,
    ln1_bias,
    qkv_weight,
    query_bias,
    value_bias,
    out_weight,
    out_bias,
    scale_attn,
    ln2_gain,
    ln2_bias,
    up_weight,
    up_bias,
    down_weight,
    down_bias,
    scale_mlp,
):
    rows, width = tokens.shape
    hidden = up_weight.shape[1]
    heads = lax.axis_size("head")
    seqs = lax.axis_size("seq")
    places = seqs // 2
    me = lax.axis_index("head")
    seq = lax.axis_index("seq")
    core = seq % 2
    place = seq // 2
    length = rows * heads
    wide = width // heads
    block = hidden // seqs
    share = width // seqs
    order = (me ^ jnp.arange(heads, dtype=jnp.int32)).astype(jnp.int32)
    groups = [[2 * i + c for i in range(places)] for c in range(2)]

    boundary = jnp.cumsum(image_counts[0])
    spots = jnp.arange(length, dtype=jnp.int32)
    labels = jnp.sum((spots[:, None] >= boundary[None, :]).astype(jnp.int32), 1)
    lab_col = labels.reshape(length, 1)
    lab_row = labels.reshape(1, length)
    line = lambda vector: vector.reshape(1, -1)

    tokens_all = lax.all_gather(tokens, "head", axis=0, tiled=True)
    grad_output = cotangent.astype(F32)
    grad_down = (scale_mlp * grad_output).astype(BF16)
    down_bias_grad = jnp.sum(grad_down.astype(F32), 0)
    grad_down_other = exchange(grad_down, "seq", 1)

    qkv, unit1 = qkv_forward(
        order,
        tokens_all,
        line(ln1_gain),
        line(ln1_bias),
        qkv_weight,
        line(query_bias),
        line(value_bias),
        heads,
        rows,
    )
    mixed_x, lse = attend(order, qkv, lab_col, lab_row, heads, rows)
    received = [exchange(mixed_x[k], "head", k) for k in range(1, heads)]
    mixed, attended, middle, normed2 = project(
        order,
        mixed_x,
        received,
        tokens,
        out_weight,
        line(out_bias),
        line(scale_attn),
        line(ln2_gain),
        line(ln2_bias),
    )
    normed2_other = exchange(normed2, "seq", 1)
    core_index = core.astype(jnp.int32).reshape(1)
    down_sum, grad_sum, up_g, down_g, up_bias_g = ffn(
        core_index,
        normed2,
        normed2_other,
        grad_down,
        grad_down_other,
        up_weight,
        line(up_bias),
        down_weight,
        places,
        block,
    )
    grad_other = exchange(grad_sum[rows:], "seq", 1)
    down_other = exchange(down_sum[rows:], "seq", 1)
    grad_middle, grad_attended, sums2, grad_x = middle_back(
        order,
        grad_sum,
        grad_other,
        cotangent,
        middle,
        attended,
        line(ln2_gain),
        line(scale_attn),
        out_weight,
        heads,
    )
    grad_received = [exchange(grad_x[k], "head", k) for k in range(1, heads)]

    downward = down_sum[:rows] + down_other + down_bias
    output = (middle + scale_mlp * downward).astype(BF16)
    scale_mlp_grad = jnp.sum(grad_output * downward, 0)

    down_part = lax.psum_scatter(down_g, "seq", scatter_dimension=0, axis_index_groups=groups, tiled=True)
    up_part = lax.psum_scatter(up_g, "seq", scatter_dimension=0, axis_index_groups=groups, tiled=True)

    split = mixed.reshape(rows, places, 2, share)
    mine = lax.dynamic_index_in_dim(split, core, 2, keepdims=False).reshape(rows, width // 2)
    theirs = lax.dynamic_index_in_dim(split, 1 - core, 2, keepdims=False).reshape(rows, width // 2)
    mixed_other = exchange(theirs, "seq", 1)
    attended_other = exchange(grad_attended, "seq", 1)
    out_g = (dot_tn(mine, grad_attended) + dot_tn(mixed_other, attended_other)).astype(BF16)
    out_blocks = out_g.reshape(places, share, width)
    out_part = pick(out_blocks, place).astype(F32)
    for j in range(1, places):
        out_part += exchange(pick(out_blocks, place ^ j), "seq", 2 * j).astype(F32)

    grad_qkv, qkv_sums = attend_back(order, grad_x, grad_received, qkv, mixed_x, lse, lab_col, lab_row)
    pieces = grad_qkv.reshape(heads, rows, 3 * wide)
    back = [exchange(pick(pieces, order[k]), "head", k) for k in range(1, heads)]
    tokens_grad = input_back(order, grad_qkv, back, qkv_weight, tokens, line(ln1_gain), grad_middle, heads)

    nothing = jnp.zeros((width,), F32)
    query_g = lax.dynamic_update_slice(nothing, qkv_sums[0, :wide], (me * wide,))
    value_g = lax.dynamic_update_slice(nothing, qkv_sums[0, 2 * wide :], (me * wide,))
    many = hidden // width
    spread = jnp.zeros((places, 2, block), F32)
    spread = lax.dynamic_update_slice(spread, up_bias_g[0].reshape(places, 1, block), (0, core, 0))
    spread = spread.reshape(seqs, many, share).transpose(1, 0, 2).reshape(many, width)
    vectors = [
        query_g,
        value_g,
        sums2[0],
        sums2[1],
        sums2[2],
        sums2[3],
        down_bias_grad,
        scale_mlp_grad,
    ]
    slots = len(vectors) + many
    small = jnp.concatenate(
        [jnp.stack(vectors), spread, jnp.zeros((128 - slots, width), F32)], 0
    )
    packed = qkv_grad(
        order,
        unit1,
        grad_qkv,
        qkv_weight,
        ln1_gain.reshape(width, 1),
        ln1_bias.reshape(width, 1),
        qkv_sums,
        small,
        slots,
        heads,
    )
    wider = 3 * wide + 128
    by_core = packed.reshape(places, 2, share, wider)
    keep = lax.dynamic_index_in_dim(by_core, core, 1, keepdims=False)
    give = lax.dynamic_index_in_dim(by_core, 1 - core, 1, keepdims=False)
    chip = (keep.astype(F32) + exchange(give, "seq", 1).astype(F32)).astype(BF16)
    total = pick(chip, place).astype(F32)
    for j in range(1, places):
        total += exchange(pick(chip, place ^ j), "seq", 2 * j).astype(F32)
    total = total.astype(BF16)
    gathered = [total] + [exchange(total, "head", k) for k in range(1, heads)]
    ordered = []
    for j in range(heads):
        choice = gathered[0]
        for k in range(1, heads):
            choice = jnp.where((me ^ k) == j, gathered[k], choice)
        ordered.append(choice)
    qkv_weight_grad = jnp.stack([item[:, : 3 * wide].reshape(share, 3, wide) for item in ordered], 2)
    qkv_weight_grad = qkv_weight_grad.reshape(share, 3 * width).astype(F32)
    columns = sum(item[:, 3 * wide :].astype(F32) for item in gathered)
    small_out = columns[:, : slots + 2].T

    up_part = up_part.reshape(-1, width)
    rest = jnp.concatenate([down_part, up_part, out_part.astype(BF16)], 0)
    rest = lax.psum(rest, "head").astype(F32)
    cut = down_part.shape[0]
    edge = cut + up_part.shape[0]
    down_weight_grad = rest[:cut]
    out_weight_grad = rest[edge:]
    up_half = rest[cut:edge].astype(BF16).reshape(2, share, places * block)
    up_mine = pick(up_half, core)
    up_theirs = exchange(pick(up_half, 1 - core), "seq", 1)
    first = jnp.where(core == 0, up_mine, up_theirs).reshape(share, places, 1, block)
    second = jnp.where(core == 0, up_theirs, up_mine).reshape(share, places, 1, block)
    up_weight_grad = jnp.concatenate([first, second], 2).reshape(share, hidden).astype(F32)

    up_bias_grad = small_out[8 : 8 + many].reshape(hidden // seqs)
    return (
        output,
        tokens_grad,
        small_out[slots],
        small_out[slots + 1],
        qkv_weight_grad,
        small_out[0],
        small_out[1],
        out_weight_grad,
        small_out[5],
        small_out[4],
        small_out[2],
        small_out[3],
        up_weight_grad,
        up_bias_grad,
        down_weight_grad,
        small_out[6],
        small_out[7],
    )


def solution(mesh):
    rows = P(("seq", "head"), None)
    flat = P("seq")
    tall = P("seq", None)
    in_specs = (rows, rows, tall) + (P(),) * 15
    out_specs = (
        rows,
        rows,
        flat,
        flat,
        tall,
        flat,
        flat,
        tall,
        flat,
        flat,
        flat,
        flat,
        tall,
        flat,
        tall,
        flat,
        flat,
    )
    return jax.shard_map(body, mesh=mesh, in_specs=in_specs, out_specs=out_specs, check_vma=False)
```
